32 devices in a mesh: ctx: 8 (over y, x, core), head: 4 (over z).
Axes of the slice: x: 2, y: 2, z: 4, core: 2. Of those that a mesh axis runs over, the one named last changes fastest.
Arguments:
- queries: bfloat16 [3072, 8192], P('ctx', 'head')
- query_scale: bfloat16 [3072, 64], P('ctx', 'head'), may hold values from 0.25 to 4
- keys: bfloat16 [3072, 1024], P('ctx', 'head')
- key_scale: bfloat16 [3072, 8], P('ctx', 'head'), may hold values from 0.4 to 2
- values: bfloat16 [3072, 1024], P('ctx', 'head'), may hold values from -6 to 6
- value_scale: bfloat16 [3072, 8], P('ctx', 'head'), may hold values from 0.5 to 2
- block_mask: int32 [24, 24], replicated, may hold values from 0 to 1, as said below
- out_weight: bfloat16 [8192, 8192], P('head'), may hold values from -0.5 to 0.5
- out_scale: float32 [8192], P('head'), may hold values from 0.5 to 2
Outputs:
- output: bfloat16 [3072, 8192], P('ctx', 'head')
The draws below stay inside these ranges and needn't reach their ends.
Inputs may be any that keep to these rules, and one draw needn't show every extreme that they name: block_mask[i, j] is 0 for j > i and 1 for j = i.
All inputs are finite; a program needn't handle non-finite values.
Results may differ from the reference program's by a relative error of at most 0.02.
Values may be sent and summed in bfloat16 or wider, within the bound.
A program may use at most 128 MiB of HBM per device.

```python
import math
import jax
import jax.numpy as jnp
from jax import lax

D = 8192
HD = 128
KEY_VALUE_HEADS = 8
GROUP = 8
BLK = 128
QH = 64
SEQUENCE_LENGTH = 3072
NBLK = 24
N_HEAD = 4


def joint_draw(key):
    key_q = jax.random.fold_in(key, 101)
    key_k = jax.random.fold_in(key, 202)
    key_qs = jax.random.fold_in(key, 303)
    key_column_blocks = jax.random.fold_in(key, 404)
    queries = jax.random.truncated_normal(key_q, -6.0, 6.0, (SEQUENCE_LENGTH, QH * HD), jnp.float32)
    keys = jax.random.truncated_normal(key_k, -6.0, 6.0, (SEQUENCE_LENGTH, KEY_VALUE_HEADS * HD), jnp.float32)
    query_dequant_scale = jnp.exp(jax.random.uniform(key_qs, (SEQUENCE_LENGTH, QH), jnp.float32, jnp.log(0.25), jnp.log(4.0)))
    key_dequant_scale = jnp.exp(jax.random.uniform(key_column_blocks, (SEQUENCE_LENGTH, KEY_VALUE_HEADS), jnp.float32, jnp.log(0.4), jnp.log(2.0)))
    return (queries, query_dequant_scale, keys, key_dequant_scale)


def draw_queries(key, part):
    return joint_draw(key)[0].astype(jnp.bfloat16)


def draw_query_scale(key, part):
    return joint_draw(key)[1].astype(jnp.bfloat16)


def draw_keys(key, part):
    return joint_draw(key)[2].astype(jnp.bfloat16)


def draw_key_scale(key, part):
    return joint_draw(key)[3].astype(jnp.bfloat16)


def draw_block_mask(key, part):
    coins = jax.random.randint(jax.random.fold_in(key, 505), (NBLK, NBLK), 0, 2, jnp.int32)
    rows = jnp.arange(NBLK, dtype=jnp.int32)[:, None]
    cols = jnp.arange(NBLK, dtype=jnp.int32)[None, :]
    table = jnp.where(cols < rows, coins, 0)
    return jnp.where(cols == rows, 1, table).astype(jnp.int32)


def shard_levels(key, extent, pieces, smallest, high):
    def one(axis_at, shards_of):
        steps = jax.random.uniform(jax.random.fold_in(jax.random.fold_in(key, 6), axis_at), (shards_of,), jnp.float32, smallest / len(pieces), high / len(pieces))
        return jnp.repeat(jnp.exp(steps), extent[axis_at] // shards_of).reshape((-1,) + (1,) * (len(extent) - axis_at - 1))

    factor_of = one(*pieces[0])
    for cut in pieces[1:]:
        factor_of = factor_of * one(*cut)
    return factor_of


def bell_draw(stream_key, shape, deviation, reach, shards=(), kind=jnp.bfloat16):
    loudness = shard_levels(stream_key, shape, shards, -0.22, 0.18) if shards else 1.0
    entries = jax.random.normal(stream_key, shape, jnp.float32) * deviation * loudness
    return jnp.minimum(jnp.maximum(entries, -reach), reach).astype(kind)


def setup_inputs(seed: int = 0) -> dict:
    arg_keys = jax.random.split(jax.random.key(seed), 10)
    queries = draw_queries(jax.random.fold_in(arg_keys[9], 71), 0)
    query_scale = draw_query_scale(jax.random.fold_in(arg_keys[9], 71), 0)
    keys = draw_keys(jax.random.fold_in(arg_keys[9], 71), 0)
    key_scale = draw_key_scale(jax.random.fold_in(arg_keys[9], 71), 0)
    values = bell_draw(arg_keys[4], (SEQUENCE_LENGTH, KEY_VALUE_HEADS * HD), 1.0, 6.0, ((0, 8), (1, 4)))
    value_scale = jnp.clip(jnp.exp(math.log(2.0) - 1.3862944 * jax.random.uniform(arg_keys[5], (SEQUENCE_LENGTH, KEY_VALUE_HEADS), jnp.float32) ** shard_levels(arg_keys[5], (SEQUENCE_LENGTH, KEY_VALUE_HEADS), ((0, 8), (1, 4)), -0.2, 0.2)), 0.5, 2.0).astype(jnp.bfloat16)
    block_mask = draw_block_mask(jax.random.fold_in(arg_keys[9], 71), 0)
    out_weight = bell_draw(arg_keys[7], (QH * HD, D), HD ** -0.5, 0.5, ((0, 4),))
    out_scale = jnp.clip(jnp.exp(math.log(2.0) - 1.3862944 * jax.random.uniform(arg_keys[8], (D,), jnp.float32) ** shard_levels(arg_keys[8], (D,), ((0, 4),), -0.2, 0.2)), 0.5, 2.0)
    return dict(queries=queries, query_scale=query_scale, keys=keys, key_scale=key_scale, values=values, value_scale=value_scale, block_mask=block_mask, out_weight=out_weight, out_scale=out_scale)


NEG_FILL = -1e+30

def reference(queries, query_scale, keys, key_scale, values, value_scale, block_mask, out_weight, out_scale):
    total_rows = queries.shape[0]
    heads_q = queries.shape[1] // HD
    kv_heads = keys.shape[1] // HD
    keys3 = keys.reshape(total_rows, kv_heads, HD).astype(jnp.float32)
    vals3 = values.reshape(total_rows, kv_heads, HD).astype(jnp.float32)
    key_sc = key_scale.astype(jnp.float32)
    val_sc = value_scale.astype(jnp.float32)
    key_pos = jnp.arange(total_rows, dtype=jnp.int32)
    key_block = key_pos // BLK
    inv_root = 1.0 / jnp.sqrt(jnp.float32(HD))

    def one_block(index):
        first = (index * BLK).astype(jnp.int32)
        q_rows = lax.dynamic_slice_in_dim(queries, first, BLK, 0).reshape(BLK, kv_heads, GROUP, HD).astype(jnp.float32)
        q_sc = lax.dynamic_slice_in_dim(query_scale, first, BLK, 0).astype(jnp.float32).reshape(BLK, kv_heads, GROUP)
        raw = jnp.einsum('rkgd,nkd->kgrn', q_rows, keys3, precision=lax.Precision.HIGHEST)
        scores = raw * jnp.transpose(q_sc, (1, 2, 0))[..., None] * key_sc.T[:, None, None, :] * inv_root
        q_pos = first + jnp.arange(BLK, dtype=jnp.int32)
        mask_row = lax.dynamic_index_in_dim(block_mask, index, 0, keepdims=False)
        block_ok = mask_row[key_block] == 1
        allowed = block_ok[None, :] & (key_pos[None, :] <= q_pos[:, None])
        scores = jnp.where(allowed[None, None], scores, NEG_FILL)
        top = lax.optimization_barrier(jnp.max(scores, axis=3))
        expo = jnp.where(allowed[None, None], jnp.exp(scores - top[..., None]), 0.0)
        total = lax.optimization_barrier(jnp.sum(expo, axis=3))
        weights = lax.optimization_barrier((expo * val_sc.T[:, None, None, :]).astype(jnp.bfloat16)).astype(jnp.float32)
        mixed = jnp.einsum('kgrn,nkd->kgrd', weights, vals3, precision=lax.Precision.HIGHEST)
        attended = mixed / total[..., None]
        return jnp.transpose(attended, (2, 0, 1, 3)).reshape(BLK, heads_q * HD).astype(jnp.bfloat16)
    blocks = lax.map(one_block, jnp.arange(total_rows // BLK, dtype=jnp.int32))
    attended = blocks.reshape(total_rows, heads_q * HD)
    rows_group = heads_q * HD // N_HEAD

    def add_group(group, summed):
        offset = (group * rows_group).astype(jnp.int32)
        cols = lax.dynamic_slice_in_dim(attended, offset, rows_group, 1)
        rows = lax.dynamic_slice_in_dim(out_weight, offset, rows_group, 0)
        part = jnp.dot(cols, rows, preferred_element_type=jnp.float32)
        part = lax.optimization_barrier(part.astype(jnp.bfloat16)).astype(jnp.float32)
        return summed + part
    summed = lax.fori_loop(0, N_HEAD, add_group, jnp.zeros((total_rows, out_weight.shape[1]), jnp.float32))
    return (summed * out_scale[None, :]).astype(jnp.bfloat16)
```

```python
import functools
import math

import jax
import jax.numpy as jnp
from jax import lax
from jax.experimental import pallas as pl
from jax.experimental.pallas import tpu as pltpu
from jax.sharding import PartitionSpec as P

HD = 128
GROUP = 8
BLK = 128
PAD_ROWS = 16
NEG_FILL = -1e30


def attend_kernel(
    per_rank, mask_ref, rank_ref, q_ref, qs_ref, k_ref, v_ref, ks_ref, o_ref, order, factor, top, accum
):
    block = rank_ref[0] * per_rank + pl.program_id(1)
    stride = per_rank * BLK + PAD_ROWS

    def note(j, count):
        @pl.when(mask_ref[block, j] == 1)
        def _():
            order[count] = j

        return count + jnp.where(mask_ref[block, j] == 1, 1, 0)

    count = lax.fori_loop(0, block, note, jnp.int32(0))
    order[count] = block
    order[count + 1] = block
    padded = lax.rem(count, 2) == 0
    pairs = count // 2 + 1

    scale = math.log2(math.e) / math.sqrt(HD)
    for h in range(GROUP):
        column = qs_ref[0, :, h : h + 1].astype(jnp.float32) * scale
        factor[h] = jnp.broadcast_to(column, (BLK, HD))
    top[...] = jnp.full_like(top, NEG_FILL)
    accum[...] = jnp.zeros_like(accum)

    def rows_of(j):
        return pl.ds(pl.multiple_of((j // per_rank) * stride + lax.rem(j, per_rank) * BLK, PAD_ROWS), BLK)

    def step(pair, last):
        a, b = order[2 * pair], order[2 * pair + 1]
        keys = jnp.concatenate([k_ref[rows_of(a), :], k_ref[rows_of(b), :]], axis=0)
        vals = jnp.concatenate([v_ref[rows_of(a), :], v_ref[rows_of(b), :]], axis=0)
        vals = jnp.concatenate([vals, jnp.ones_like(vals)], axis=1)
        lanes = [pl.ds(pl.multiple_of(j * BLK, BLK), BLK) for j in (a, b)]
        key_sc = jnp.concatenate([ks_ref[0, :, lanes[0]], ks_ref[0, :, lanes[1]]], axis=1)
        if last:
            row = lax.broadcasted_iota(jnp.int32, (BLK, 2 * BLK), 0)
            col = lax.broadcasted_iota(jnp.int32, (BLK, 2 * BLK), 1)
            first_ok = jnp.where(padded, 0, BLK)
            allowed = (col < first_ok) | ((col >= BLK) & (col - BLK <= row))
        for h in range(GROUP):
            raw = lax.dot_general(
                q_ref[:, h * HD : (h + 1) * HD],
                keys,
                (((1,), (1,)), ((), ())),
                preferred_element_type=jnp.float32,
            )
            x = raw * key_sc
            if last:
                x = jnp.where(allowed, x, NEG_FILL)
            old = top[h]
            new = jnp.maximum(old, jnp.max(x, axis=1, keepdims=True))
            fac = factor[h]
            decay = jnp.exp2((old - new) * fac)
            expo = jnp.exp2(
                (x - jnp.concatenate([new, new], axis=1)) * jnp.concatenate([fac, fac], axis=1)
            )
            top[h] = new
            accum[h] = accum[h] * jnp.concatenate([decay, decay], axis=1) + jnp.dot(
                expo.astype(jnp.bfloat16), vals, preferred_element_type=jnp.float32
            )

    @pl.loop(0, pairs - 1)
    def _(pair):
        step(pair, False)

    step(pairs - 1, True)
    for h in range(GROUP):
        o_ref[:, h * HD : (h + 1) * HD] = (accum[h, :, :HD] / accum[h, :, HD:]).astype(jnp.bfloat16)


def attend(queries, query_scale, packed, key_sc, block_mask, rank):
    rows, width = queries.shape
    kv_local = width // (GROUP * HD)
    per_rank = rows // BLK
    count = block_mask.shape[0]
    q_sc = jnp.transpose(query_scale.reshape(rows, kv_local, GROUP), (1, 0, 2))
    return pl.pallas_call(
        functools.partial(attend_kernel, per_rank),
        out_shape=jax.ShapeDtypeStruct((rows, width), jnp.bfloat16),
        grid_spec=pltpu.PrefetchScalarGridSpec(
            num_scalar_prefetch=2,
            grid=(kv_local, per_rank),
            in_specs=[
                pl.BlockSpec((BLK, GROUP * HD), lambda g, i, *_: (i, g)),
                pl.BlockSpec((1, BLK, GROUP), lambda g, i, *_: (g, i, 0)),
                pl.BlockSpec((packed.shape[0], HD), lambda g, i, *_: (0, g)),
                pl.BlockSpec((packed.shape[0], HD), lambda g, i, *_: (0, kv_local + g)),
                pl.BlockSpec((1, 1, count * BLK), lambda g, i, *_: (g, 0, 0)),
            ],
            out_specs=pl.BlockSpec((BLK, GROUP * HD), lambda g, i, *_: (i, g)),
            scratch_shapes=[
                pltpu.SMEM((count + 2,), jnp.int32),
                pltpu.VMEM((GROUP, BLK, HD), jnp.float32),
                pltpu.VMEM((GROUP, BLK, HD), jnp.float32),
                pltpu.VMEM((GROUP, BLK, 2 * HD), jnp.float32),
            ],
        ),
        compiler_params=pltpu.CompilerParams(vmem_limit_bytes=24 * 2**20),
    )(block_mask, rank.reshape(1), queries, q_sc, packed, packed, key_sc)


def local(
    queries, query_scale, keys, key_scale, values, value_scale, block_mask, out_weight, out_scale
):
    rows = queries.shape[0]
    kv_local = keys.shape[1] // HD
    rank = lax.axis_index("ctx").astype(jnp.int32)
    scaled = (
        values.reshape(rows, kv_local, HD).astype(jnp.float32)
        * value_scale.astype(jnp.float32)[..., None]
    ).astype(jnp.bfloat16).reshape(rows, kv_local * HD)
    width = 2 * kv_local * HD
    slots = kv_local * (rows // BLK)
    tail = jnp.pad(key_scale.T.reshape(slots, BLK), ((0, PAD_ROWS - slots), (0, width - BLK)))
    packed = jnp.concatenate([jnp.concatenate([keys, scaled], axis=1), tail], axis=0)
    gathered = lax.all_gather(packed, "ctx", axis=0, tiled=True)
    ranks = gathered.shape[0] // packed.shape[0]
    key_sc = gathered.reshape(ranks, rows + PAD_ROWS, width)[:, rows : rows + slots, :BLK]
    key_sc = jnp.transpose(key_sc.astype(jnp.float32).reshape(ranks, kv_local, rows), (1, 0, 2))
    key_sc = key_sc.reshape(kv_local, 1, ranks * rows)
    attended = attend(queries, query_scale, gathered, key_sc, block_mask, rank)
    projected = jnp.dot(attended, out_weight, preferred_element_type=jnp.float32)
    summed = lax.psum_scatter(
        projected.astype(jnp.bfloat16), "head", scatter_dimension=1, tiled=True
    ).astype(jnp.float32)
    return (summed * out_scale[None, :]).astype(jnp.bfloat16)


def solution(mesh):
    return jax.shard_map(
        local,
        mesh=mesh,
        in_specs=(
            P("ctx", "head"),
            P("ctx", "head"),
            P("ctx", "head"),
            P("ctx", "head"),
            P("ctx", "head"),
            P("ctx", "head"),
            P(),
            P("head", None),
            P("head"),
        ),
        out_specs=P("ctx", "head"),
        check_vma=False,
    )
```

```python
import functools
import math

import jax
import jax.numpy as jnp
from jax import lax
from jax.experimental import pallas as pl
from jax.experimental.pallas import tpu as pltpu
from jax.sharding import PartitionSpec as P

HD = 128
GROUP = 8
BLK = 128
PAD_ROWS = 16
NEG_FILL = -1e30


def attend_kernel(
    per_rank, mask_ref, rank_ref, q_ref, qs_ref, k_ref, v_ref, ks_ref, o_ref, order, factor, top, accum
):
    block = rank_ref[0] * per_rank + pl.program_id(1)
    stride = per_rank * BLK + PAD_ROWS

    def note(j, count):
        @pl.when(mask_ref[block, j] == 1)
        def _():
            order[count] = j

        return count + jnp.where(mask_ref[block, j] == 1, 1, 0)

    count = lax.fori_loop(0, block, note, jnp.int32(0))
    order[count] = block
    order[count + 1] = block
    padded = lax.rem(count, 2) == 0
    pairs = count // 2 + 1

    scale = math.log2(math.e) / math.sqrt(HD)
    for h in range(GROUP):
        column = qs_ref[0, :, h : h + 1].astype(jnp.float32) * scale
        factor[h] = jnp.broadcast_to(column, (BLK, HD))
    top[...] = jnp.full_like(top, NEG_FILL)
    accum[...] = jnp.zeros_like(accum)

    def rows_of(j):
        return pl.ds(pl.multiple_of((j // per_rank) * stride + lax.rem(j, per_rank) * BLK, PAD_ROWS), BLK)

    def step(pair, last):
        a, b = order[2 * pair], order[2 * pair + 1]
        keys = jnp.concatenate([k_ref[rows_of(a), :], k_ref[rows_of(b), :]], axis=0)
        vals = jnp.concatenate([v_ref[rows_of(a), :], v_ref[rows_of(b), :]], axis=0)
        vals = jnp.concatenate([vals, jnp.ones_like(vals)], axis=1)
        lanes = [pl.ds(pl.multiple_of(j * BLK, BLK), BLK) for j in (a, b)]
        key_sc = jnp.concatenate([ks_ref[0, :, lanes[0]], ks_ref[0, :, lanes[1]]], axis=1)
        if last:
            row = lax.broadcasted_iota(jnp.int32, (BLK, 2 * BLK), 0)
            col = lax.broadcasted_iota(jnp.int32, (BLK, 2 * BLK), 1)
            first_ok = jnp.where(padded, 0, BLK)
            allowed = (col < first_ok) | ((col >= BLK) & (col - BLK <= row))
        for h in range(GROUP):
            raw = lax.dot_general(
                q_ref[:, h * HD : (h + 1) * HD],
                keys,
                (((1,), (1,)), ((), ())),
                preferred_element_type=jnp.float32,
            )
            x = raw * key_sc
            if last:
                x = jnp.where(allowed, x, NEG_FILL)
            old = top[h]
            new = jnp.maximum(old, jnp.max(x, axis=1, keepdims=True))
            fac = factor[h]
            decay = jnp.exp2((old - new) * fac)
            expo = jnp.exp2(
                (x - jnp.concatenate([new, new], axis=1)) * jnp.concatenate([fac, fac], axis=1)
            )
            top[h] = new
            accum[h] = accum[h] * jnp.concatenate([decay, decay], axis=1) + jnp.dot(
                expo.astype(jnp.bfloat16), vals, preferred_element_type=jnp.float32
            )

    @pl.loop(0, pairs - 1)
    def _(pair):
        step(pair, False)

    step(pairs - 1, True)
    for h in range(GROUP):
        o_ref[:, h * HD : (h + 1) * HD] = (accum[h, :, :HD] / accum[h, :, HD:]).astype(jnp.bfloat16)


def attend(queries, q_sc, packed, key_sc, block_mask, rank, blocks):
    rows, width = queries.shape
    kv_local = width // (GROUP * HD)
    per_rank = rows // BLK
    count = block_mask.shape[0]
    return pl.pallas_call(
        functools.partial(attend_kernel, per_rank),
        out_shape=jax.ShapeDtypeStruct((blocks * BLK, width), jnp.bfloat16),
        grid_spec=pltpu.PrefetchScalarGridSpec(
            num_scalar_prefetch=2,
            grid=(kv_local, blocks),
            in_specs=[
                pl.BlockSpec((BLK, GROUP * HD), lambda g, i, *_: (i, g)),
                pl.BlockSpec((1, BLK, GROUP), lambda g, i, *_: (g, i, 0)),
                pl.BlockSpec((packed.shape[0], HD), lambda g, i, *_: (0, g)),
                pl.BlockSpec((packed.shape[0], HD), lambda g, i, *_: (0, kv_local + g)),
                pl.BlockSpec((1, 1, count * BLK), lambda g, i, *_: (g, 0, 0)),
            ],
            out_specs=pl.BlockSpec((BLK, GROUP * HD), lambda g, i, *_: (i, g)),
            scratch_shapes=[
                pltpu.SMEM((count + 2,), jnp.int32),
                pltpu.VMEM((GROUP, BLK, HD), jnp.float32),
                pltpu.VMEM((GROUP, BLK, HD), jnp.float32),
                pltpu.VMEM((GROUP, BLK, 2 * HD), jnp.float32),
            ],
        ),
        compiler_params=pltpu.CompilerParams(vmem_limit_bytes=24 * 2**20),
    )(block_mask, rank.reshape(1), queries, q_sc, packed, packed, key_sc)


def project_kernel(
    n,
    ranks,
    first_ref,
    q_ref,
    qs_ref,
    kv_ref,
    ks_ref,
    mask_ref,
    w_hbm,
    scale_ref,
    o_ref,
    weight,
    attended,
    parts,
    factor,
    top,
    accum,
    w_sem,
    send_sem,
    recv_sem,
):
    me = lax.axis_index("head")
    rank = lax.axis_index("ctx")
    chunks = attended.shape[0]
    done = first_ref.shape[0] // BLK
    kv_local = qs_ref.shape[0]
    stride = chunks * BLK + PAD_ROWS
    features = weight.shape[2]
    tile = math.gcd(features, 512)
    is_end = (me == 0) | (me == n - 1)

    def load_weight(d):
        return pltpu.make_async_copy(
            w_hbm.at[:, pl.ds(pl.multiple_of(d * features, features), features)],
            weight.at[d],
            w_sem.at[d],
        )

    for s in range(n):
        d = jnp.where(me < (n + 1) // 2, n - 1 - s, s)
        load_weight(d).start()

    barrier = pltpu.get_barrier_semaphore()

    @pl.when(me > 0)
    def _():
        pl.semaphore_signal(
            barrier, inc=1, device_id={"head": me - 1}, device_id_type=pl.DeviceIdType.MESH
        )

    @pl.when(me < n - 1)
    def _():
        pl.semaphore_signal(
            barrier, inc=1, device_id={"head": me + 1}, device_id_type=pl.DeviceIdType.MESH
        )

    @pl.when(is_end)
    def _():
        pl.semaphore_wait(barrier, 1)

    @pl.when(jnp.logical_not(is_end))
    def _():
        pl.semaphore_wait(barrier, 2)

    for c in range(done):
        attended[c] = first_ref[c * BLK : (c + 1) * BLK, :]

    def attend_chunk(t):
        block = rank * chunks + t
        q_rows = pl.ds(pl.multiple_of(t * BLK, BLK), BLK)
        scale = math.log2(math.e) / math.sqrt(HD)

        @pl.loop(0, kv_local)
        def _(g):
            for h in range(GROUP):
                column = qs_ref[g, q_rows, h : h + 1].astype(jnp.float32) * scale
                factor[h] = jnp.broadcast_to(column, (BLK, HD))
            top[...] = jnp.full_like(top, NEG_FILL)
            accum[...] = jnp.zeros_like(accum)

            @pl.loop(0, block // 2 + 1)
            def _(pair):
                a = 2 * pair
                b = jnp.minimum(a + 1, ranks * chunks - 1)

                def piece(j, column):
                    begin = (j // chunks) * stride + lax.rem(j, chunks) * BLK
                    return kv_ref[
                        pl.ds(pl.multiple_of(begin, PAD_ROWS), BLK),
                        pl.ds(pl.multiple_of(column * HD, HD), HD),
                    ]

                def lanes(j):
                    return pl.ds(pl.multiple_of(j * BLK, BLK), BLK)

                keys = jnp.concatenate([piece(a, g), piece(b, g)], axis=0)
                vals = jnp.concatenate([piece(a, kv_local + g), piece(b, kv_local + g)], axis=0)
                vals = jnp.concatenate([vals, jnp.ones_like(vals)], axis=1)
                key_sc = jnp.concatenate([ks_ref[g, :, lanes(a)], ks_ref[g, :, lanes(b)]], axis=1)
                read = jnp.concatenate([mask_ref[t, :, lanes(a)], mask_ref[t, :, lanes(b)]], axis=1)
                row = lax.broadcasted_iota(jnp.int32, (BLK, 2 * BLK), 0) + block * BLK
                col = lax.broadcasted_iota(jnp.int32, (BLK, 2 * BLK), 1) + a * BLK
                allowed = (jnp.broadcast_to(read, (BLK, 2 * BLK)) == 1) & (col <= row)
                for h in range(GROUP):
                    column = pl.multiple_of((g * GROUP + h) * HD, HD)
                    raw = lax.dot_general(
                        q_ref[q_rows, pl.ds(column, HD)],
                        keys,
                        (((1,), (1,)), ((), ())),
                        preferred_element_type=jnp.float32,
                    )
                    x = jnp.where(allowed, raw * key_sc, NEG_FILL)
                    old = top[h]
                    new = jnp.maximum(old, jnp.max(x, axis=1, keepdims=True))
                    fac = factor[h]
                    decay = jnp.exp2((old - new) * fac)
                    expo = jnp.exp2(
                        (x - jnp.concatenate([new, new], axis=1))
                        * jnp.concatenate([fac, fac], axis=1)
                    )
                    top[h] = new
                    accum[h] = accum[h] * jnp.concatenate([decay, decay], axis=1) + jnp.dot(
                        expo.astype(jnp.bfloat16), vals, preferred_element_type=jnp.float32
                    )

            for h in range(GROUP):
                column = pl.multiple_of((g * GROUP + h) * HD, HD)
                attended[t, :, pl.ds(column, HD)] = (
                    accum[h, :, :HD] / accum[h, :, HD:]
                ).astype(jnp.bfloat16)

    def products(c, d, use):
        @pl.loop(0, features // tile)
        def _(i):
            cols = pl.ds(pl.multiple_of(i * tile, tile), tile)
            use(
                cols,
                jnp.dot(attended[c], weight[d, :, cols], preferred_element_type=jnp.float32),
            )

    def hop(c, d, up):
        slot = d if up else jnp.where(d == me - 1, n, d)
        return pltpu.make_async_remote_copy(
            src_ref=parts.at[c, d],
            dst_ref=parts.at[c, slot],
            send_sem=send_sem.at[c, d],
            recv_sem=recv_sem.at[c, slot],
            device_id={"head": me + 1 if up else me - 1},
            device_id_type=pl.DeviceIdType.MESH,
        )

    def arrived(c, slot):
        pltpu.make_async_copy(parts.at[c, slot], parts.at[c, slot], recv_sem.at[c, slot]).wait()

    def relay(c, d, up):
        source = me > 0 if up else me < n - 1

        @pl.when(c == 0)
        def _():
            load_weight(d).wait()

        @pl.when(source)
        def _():
            arrived(c, d)

            def use(cols, product):
                parts[c, d, :, cols] = (parts[c, d, :, cols].astype(jnp.float32) + product).astype(
                    jnp.bfloat16
                )

            products(c, d, use)

        @pl.when(jnp.logical_not(source))
        def _():
            def use(cols, product):
                parts[c, d, :, cols] = product.astype(jnp.bfloat16)

            products(c, d, use)

        hop(c, d, up).start()

    def forward(c):
        @pl.loop(0, n - 1)
        def _(s):
            @pl.when(n - 1 - s > me)
            def _():
                relay(c, n - 1 - s, True)

            @pl.when(s < me)
            def _():
                relay(c, s, False)

    @pl.loop(0, chunks)
    def _(t):
        @pl.when(t >= done)
        def _():
            attend_chunk(t)

        @pl.when(is_end)
        def _():
            forward(t)

        @pl.when(jnp.logical_not(is_end) & (t > 0))
        def _():
            forward(t - 1)

    @pl.when(jnp.logical_not(is_end))
    def _():
        forward(chunks - 1)

    load_weight(me).wait()

    @pl.loop(0, chunks)
    def _(c):
        rows = pl.ds(pl.multiple_of(c * BLK, BLK), BLK)

        def finish(below, above):
            if below:
                arrived(c, me)
            if above:
                arrived(c, n)

            def use(cols, product):
                if below:
                    product = product + parts[c, me, :, cols].astype(jnp.float32)
                if above:
                    product = product + parts[c, n, :, cols].astype(jnp.float32)
                o_ref[rows, cols] = (product * scale_ref[:, cols]).astype(jnp.bfloat16)

            products(c, me, use)

        @pl.when(me == 0)
        def _():
            finish(False, True)

        @pl.when(me == n - 1)
        def _():
            finish(True, False)

        @pl.when(jnp.logical_not(is_end))
        def _():
            finish(True, True)

        for d in range(n):

            @pl.when(d > me)
            def _():
                hop(c, d, True).wait_send()

            @pl.when(d < me)
            def _():
                hop(c, d, False).wait_send()


def project(first, queries, q_sc, packed, key_sc, mask_rows, out_weight, out_scale):
    n = lax.axis_size("head")
    ranks = lax.axis_size("ctx")
    rows, width = queries.shape
    chunks = rows // BLK
    features = out_weight.shape[1] // n
    vmem = pl.BlockSpec(memory_space=pltpu.VMEM)
    return pl.pallas_call(
        functools.partial(project_kernel, n, ranks),
        out_shape=jax.ShapeDtypeStruct((rows, features), jnp.bfloat16),
        in_specs=[vmem] * 6 + [pl.BlockSpec(memory_space=pl.ANY), vmem],
        out_specs=vmem,
        scratch_shapes=[
            pltpu.VMEM((n, width, features), jnp.bfloat16),
            pltpu.VMEM((chunks, BLK, width), jnp.bfloat16),
            pltpu.VMEM((chunks, n + 1, BLK, features), jnp.bfloat16),
            pltpu.VMEM((GROUP, BLK, HD), jnp.float32),
            pltpu.VMEM((GROUP, BLK, HD), jnp.float32),
            pltpu.VMEM((GROUP, BLK, 2 * HD), jnp.float32),
            pltpu.SemaphoreType.DMA((n,)),
            pltpu.SemaphoreType.DMA((chunks, n)),
            pltpu.SemaphoreType.DMA((chunks, n + 1)),
        ],
        compiler_params=pltpu.CompilerParams(
            collective_id=0, has_side_effects=True, vmem_limit_bytes=60 * 2**20
        ),
    )(first, queries, q_sc, packed, key_sc, mask_rows, out_weight, out_scale.reshape(1, -1))


def local(
    queries, query_scale, keys, key_scale, values, value_scale, block_mask, out_weight, out_scale
):
    rows = queries.shape[0]
    kv_local = keys.shape[1] // HD
    rank = lax.axis_index("ctx").astype(jnp.int32)
    scaled = (
        values.reshape(rows, kv_local, HD).astype(jnp.float32)
        * value_scale.astype(jnp.float32)[..., None]
    ).astype(jnp.bfloat16).reshape(rows, kv_local * HD)
    width = 2 * kv_local * HD
    slots = kv_local * (rows // BLK)
    tail = jnp.pad(key_scale.T.reshape(slots, BLK), ((0, PAD_ROWS - slots), (0, width - BLK)))
    packed = jnp.concatenate([jnp.concatenate([keys, scaled], axis=1), tail], axis=0)
    gathered = lax.all_gather(packed, "ctx", axis=0, tiled=True)
    ranks = gathered.shape[0] // packed.shape[0]
    key_sc = gathered.reshape(ranks, rows + PAD_ROWS, width)[:, rows : rows + slots, :BLK]
    key_sc = jnp.transpose(key_sc.astype(jnp.float32).reshape(ranks, kv_local, rows), (1, 0, 2))
    key_sc = key_sc.reshape(kv_local, 1, ranks * rows)
    q_sc = jnp.transpose(query_scale.reshape(rows, kv_local, GROUP), (1, 0, 2))
    own = lax.dynamic_slice_in_dim(block_mask, rank * (rows // BLK), rows // BLK, 0)
    mask_rows = jnp.repeat(own, BLK, axis=1)[:, None, :]
    first = attend(queries, q_sc, gathered, key_sc, block_mask, rank, 1)
    return project(first, queries, q_sc, gathered, key_sc, mask_rows, out_weight, out_scale)


def solution(mesh):
    return jax.shard_map(
        local,
        mesh=mesh,
        in_specs=(
            P("ctx", "head"),
            P("ctx", "head"),
            P("ctx", "head"),
            P("ctx", "head"),
            P("ctx", "head"),
            P("ctx", "head"),
            P(),
            P("head", None),
            P("head"),
        ),
        out_specs=P("ctx", "head"),
        check_vma=False,
    )
```

```python
import functools
import math

import jax
import jax.numpy as jnp
from jax import lax
from jax.experimental import pallas as pl
from jax.experimental.pallas import tpu as pltpu
from jax.sharding import PartitionSpec as P

HD = 128
GROUP = 8
BLK = 128
PAD_ROWS = 16
DEPTH = 2
NEG_FILL = -1e30


def attend_kernel(
    per_rank, mask_ref, rank_ref, q_ref, qs_ref, k_ref, v_ref, ks_ref, o_ref, order, factor, top, accum
):
    block = rank_ref[0] * per_rank + pl.program_id(1)
    stride = per_rank * BLK + PAD_ROWS

    def note(j, count):
        @pl.when(mask_ref[block, j] == 1)
        def _():
            order[count] = j

        return count + jnp.where(mask_ref[block, j] == 1, 1, 0)

    count = lax.fori_loop(0, block, note, jnp.int32(0))
    order[count] = block
    order[count + 1] = block
    padded = lax.rem(count, 2) == 0
    pairs = count // 2 + 1

    scale = math.log2(math.e) / math.sqrt(HD)
    for h in range(GROUP):
        column = qs_ref[0, :, h : h + 1].astype(jnp.float32) * scale
        factor[h] = jnp.broadcast_to(column, (BLK, HD))
    top[...] = jnp.full_like(top, NEG_FILL)
    accum[...] = jnp.zeros_like(accum)

    def rows_of(j):
        return pl.ds(pl.multiple_of((j // per_rank) * stride + lax.rem(j, per_rank) * BLK, PAD_ROWS), BLK)

    def step(pair, last):
        a, b = order[2 * pair], order[2 * pair + 1]
        keys = jnp.concatenate([k_ref[rows_of(a), :], k_ref[rows_of(b), :]], axis=0)
        vals = jnp.concatenate([v_ref[rows_of(a), :], v_ref[rows_of(b), :]], axis=0)
        vals = jnp.concatenate([vals, jnp.ones_like(vals)], axis=1)
        lanes = [pl.ds(pl.multiple_of(j * BLK, BLK), BLK) for j in (a, b)]
        key_sc = jnp.concatenate([ks_ref[0, :, lanes[0]], ks_ref[0, :, lanes[1]]], axis=1)
        if last:
            row = lax.broadcasted_iota(jnp.int32, (BLK, 2 * BLK), 0)
            col = lax.broadcasted_iota(jnp.int32, (BLK, 2 * BLK), 1)
            first_ok = jnp.where(padded, 0, BLK)
            allowed = (col < first_ok) | ((col >= BLK) & (col - BLK <= row))
        for h in range(GROUP):
            raw = lax.dot_general(
                q_ref[:, h * HD : (h + 1) * HD],
                keys,
                (((1,), (1,)), ((), ())),
                preferred_element_type=jnp.float32,
            )
            x = raw * key_sc
            if last:
                x = jnp.where(allowed, x, NEG_FILL)
            old = top[h]
            new = jnp.maximum(old, jnp.max(x, axis=1, keepdims=True))
            fac = factor[h]
            decay = jnp.exp2((old - new) * fac)
            expo = jnp.exp2(
                (x - jnp.concatenate([new, new], axis=1)) * jnp.concatenate([fac, fac], axis=1)
            )
            top[h] = new
            accum[h] = accum[h] * jnp.concatenate([decay, decay], axis=1) + jnp.dot(
                expo.astype(jnp.bfloat16), vals, preferred_element_type=jnp.float32
            )

    @pl.loop(0, pairs - 1)
    def _(pair):
        step(pair, False)

    step(pairs - 1, True)
    for h in range(GROUP):
        o_ref[:, h * HD : (h + 1) * HD] = (accum[h, :, :HD] / accum[h, :, HD:]).astype(jnp.bfloat16)


def attend(queries, q_sc, packed, key_sc, block_mask, rank, blocks):
    rows, width = queries.shape
    kv_local = width // (GROUP * HD)
    per_rank = rows // BLK
    count = block_mask.shape[0]
    return pl.pallas_call(
        functools.partial(attend_kernel, per_rank),
        out_shape=jax.ShapeDtypeStruct((blocks * BLK, width), jnp.bfloat16),
        grid_spec=pltpu.PrefetchScalarGridSpec(
            num_scalar_prefetch=2,
            grid=(kv_local, blocks),
            in_specs=[
                pl.BlockSpec((BLK, GROUP * HD), lambda g, i, *_: (i, g)),
                pl.BlockSpec((1, BLK, GROUP), lambda g, i, *_: (g, i, 0)),
                pl.BlockSpec((packed.shape[0], HD), lambda g, i, *_: (0, g)),
                pl.BlockSpec((packed.shape[0], HD), lambda g, i, *_: (0, kv_local + g)),
                pl.BlockSpec((1, 1, count * BLK), lambda g, i, *_: (g, 0, 0)),
            ],
            out_specs=pl.BlockSpec((BLK, GROUP * HD), lambda g, i, *_: (i, g)),
            scratch_shapes=[
                pltpu.SMEM((count + 2,), jnp.int32),
                pltpu.VMEM((GROUP, BLK, HD), jnp.float32),
                pltpu.VMEM((GROUP, BLK, HD), jnp.float32),
                pltpu.VMEM((GROUP, BLK, 2 * HD), jnp.float32),
            ],
        ),
        compiler_params=pltpu.CompilerParams(vmem_limit_bytes=24 * 2**20),
    )(block_mask, rank.reshape(1), queries, q_sc, packed, packed, key_sc)


def project_kernel(
    n,
    ranks,
    first_ref,
    q_ref,
    qs_ref,
    kv_ref,
    ks_ref,
    mask_ref,
    w_hbm,
    scale_ref,
    o_ref,
    weight,
    attended,
    parts,
    factor,
    top,
    accum,
    w_sem,
    send_sem,
    recv_sem,
):
    me = lax.axis_index("head")
    rank = lax.axis_index("ctx")
    chunks = attended.shape[0]
    done = first_ref.shape[0] // BLK
    kv_local = qs_ref.shape[0]
    stride = chunks * BLK + PAD_ROWS
    features = weight.shape[2]
    tile = math.gcd(features, 512)
    is_end = (me == 0) | (me == n - 1)

    def load_weight(d):
        return pltpu.make_async_copy(
            w_hbm.at[:, pl.ds(pl.multiple_of(d * features, features), features)],
            weight.at[d],
            w_sem.at[d],
        )

    for s in range(n):
        d = jnp.where(me < (n + 1) // 2, n - 1 - s, s)
        load_weight(d).start()

    barrier = pltpu.get_barrier_semaphore()

    @pl.when(me > 0)
    def _():
        pl.semaphore_signal(
            barrier, inc=1, device_id={"head": me - 1}, device_id_type=pl.DeviceIdType.MESH
        )

    @pl.when(me < n - 1)
    def _():
        pl.semaphore_signal(
            barrier, inc=1, device_id={"head": me + 1}, device_id_type=pl.DeviceIdType.MESH
        )

    @pl.when(is_end)
    def _():
        pl.semaphore_wait(barrier, 1)

    @pl.when(jnp.logical_not(is_end))
    def _():
        pl.semaphore_wait(barrier, 2)

    for c in range(done):
        attended[c] = first_ref[c * BLK : (c + 1) * BLK, :]

    def attend_chunk(t):
        block = rank * chunks + t
        q_rows = pl.ds(pl.multiple_of(t * BLK, BLK), BLK)
        scale = math.log2(math.e) / math.sqrt(HD)

        @pl.loop(0, kv_local)
        def _(g):
            for h in range(GROUP):
                column = qs_ref[g, q_rows, h : h + 1].astype(jnp.float32) * scale
                factor[h] = jnp.broadcast_to(column, (BLK, HD))
            top[...] = jnp.full_like(top, NEG_FILL)
            accum[...] = jnp.zeros_like(accum)

            @pl.loop(0, block // 2 + 1)
            def _(pair):
                a = 2 * pair
                b = jnp.minimum(a + 1, ranks * chunks - 1)

                def piece(j, column):
                    begin = (j // chunks) * stride + lax.rem(j, chunks) * BLK
                    return kv_ref[
                        pl.ds(pl.multiple_of(begin, PAD_ROWS), BLK),
                        pl.ds(pl.multiple_of(column * HD, HD), HD),
                    ]

                def lanes(j):
                    return pl.ds(pl.multiple_of(j * BLK, BLK), BLK)

                keys = jnp.concatenate([piece(a, g), piece(b, g)], axis=0)
                vals = jnp.concatenate([piece(a, kv_local + g), piece(b, kv_local + g)], axis=0)
                vals = jnp.concatenate([vals, jnp.ones_like(vals)], axis=1)
                key_sc = jnp.concatenate([ks_ref[g, :, lanes(a)], ks_ref[g, :, lanes(b)]], axis=1)
                read = jnp.concatenate([mask_ref[t, :, lanes(a)], mask_ref[t, :, lanes(b)]], axis=1)
                row = lax.broadcasted_iota(jnp.int32, (BLK, 2 * BLK), 0) + block * BLK
                col = lax.broadcasted_iota(jnp.int32, (BLK, 2 * BLK), 1) + a * BLK
                allowed = (jnp.broadcast_to(read, (BLK, 2 * BLK)) == 1) & (col <= row)
                for h in range(GROUP):
                    column = pl.multiple_of((g * GROUP + h) * HD, HD)
                    raw = lax.dot_general(
                        q_ref[q_rows, pl.ds(column, HD)],
                        keys,
                        (((1,), (1,)), ((), ())),
                        preferred_element_type=jnp.float32,
                    )
                    x = jnp.where(allowed, raw * key_sc, NEG_FILL)
                    old = top[h]
                    new = jnp.maximum(old, jnp.max(x, axis=1, keepdims=True))
                    fac = factor[h]
                    decay = jnp.exp2((old - new) * fac)
                    expo = jnp.exp2(
                        (x - jnp.concatenate([new, new], axis=1))
                        * jnp.concatenate([fac, fac], axis=1)
                    )
                    top[h] = new
                    accum[h] = accum[h] * jnp.concatenate([decay, decay], axis=1) + jnp.dot(
                        expo.astype(jnp.bfloat16), vals, preferred_element_type=jnp.float32
                    )

            for h in range(GROUP):
                column = pl.multiple_of((g * GROUP + h) * HD, HD)
                attended[t, :, pl.ds(column, HD)] = (
                    accum[h, :, :HD] / accum[h, :, HD:]
                ).astype(jnp.bfloat16)

    def products(c, d, use):
        @pl.loop(0, features // tile)
        def _(i):
            cols = pl.ds(pl.multiple_of(i * tile, tile), tile)
            use(
                cols,
                jnp.dot(attended[c], weight[d, :, cols], preferred_element_type=jnp.float32),
            )

    def hop(c, d, up):
        slot = d if up else jnp.where(d == me - 1, n, d)
        return pltpu.make_async_remote_copy(
            src_ref=parts.at[c, d],
            dst_ref=parts.at[c, slot],
            send_sem=send_sem.at[c, d],
            recv_sem=recv_sem.at[c, slot],
            device_id={"head": me + 1 if up else me - 1},
            device_id_type=pl.DeviceIdType.MESH,
        )

    def arrived(c, slot):
        pltpu.make_async_copy(parts.at[c, slot], parts.at[c, slot], recv_sem.at[c, slot]).wait()

    def count_of(up):
        return n - 1 - me if up else me

    def nth(q, up):
        per = jnp.maximum(count_of(up), 1)
        k = lax.rem(q, per)
        return hop(lax.div(q, per), n - 1 - k if up else k, up)

    def relay(c, k, up):
        d = n - 1 - k if up else k
        source = me > 0 if up else me < n - 1

        @pl.when(c == 0)
        def _():
            load_weight(d).wait()

        @pl.when(source)
        def _():
            arrived(c, d)

            def use(cols, product):
                parts[c, d, :, cols] = (parts[c, d, :, cols].astype(jnp.float32) + product).astype(
                    jnp.bfloat16
                )

            products(c, d, use)

        @pl.when(jnp.logical_not(source))
        def _():
            def use(cols, product):
                parts[c, d, :, cols] = product.astype(jnp.bfloat16)

            products(c, d, use)

        q = c * count_of(up) + k

        @pl.when(q >= DEPTH)
        def _():
            nth(q - DEPTH, up).wait_send()

        nth(q, up).start()

    def forward(c):
        def ups():
            @pl.loop(0, n - 1 - me)
            def _(k):
                relay(c, k, True)

        def downs():
            @pl.loop(0, me)
            def _(k):
                relay(c, k, False)

        @pl.when(me < n // 2)
        def _():
            ups()
            downs()

        @pl.when(me >= n // 2)
        def _():
            downs()
            ups()

    @pl.loop(0, chunks)
    def _(t):
        @pl.when(t >= done)
        def _():
            attend_chunk(t)

        @pl.when(is_end)
        def _():
            forward(t)

        @pl.when(jnp.logical_not(is_end) & (t > 0))
        def _():
            forward(t - 1)

    @pl.when(jnp.logical_not(is_end))
    def _():
        forward(chunks - 1)

    load_weight(me).wait()

    @pl.loop(0, chunks)
    def _(c):
        rows = pl.ds(pl.multiple_of(c * BLK, BLK), BLK)

        def finish(below, above):
            if below:
                arrived(c, me)
            if above:
                arrived(c, n)

            def use(cols, product):
                if below:
                    product = product + parts[c, me, :, cols].astype(jnp.float32)
                if above:
                    product = product + parts[c, n, :, cols].astype(jnp.float32)
                o_ref[rows, cols] = (product * scale_ref[:, cols]).astype(jnp.bfloat16)

            products(c, me, use)

        @pl.when(me == 0)
        def _():
            finish(False, True)

        @pl.when(me == n - 1)
        def _():
            finish(True, False)

        @pl.when(jnp.logical_not(is_end))
        def _():
            finish(True, True)

    for up in (True, False):
        total = chunks * count_of(up)

        @pl.loop(jnp.maximum(total - DEPTH, 0), total)
        def _(q):
            nth(q, up).wait_send()


def gather_kernel(ranks, x_ref, o_ref, own_sem, send_sem, pass_sem, recv_sem):
    rank = lax.axis_index("ctx")
    chips = ranks // 2
    other = rank + 1 - 2 * lax.rem(rank, 2)

    def send(src, slot, sem, target):
        return pltpu.make_async_remote_copy(
            src_ref=src,
            dst_ref=o_ref.at[slot],
            send_sem=sem,
            recv_sem=recv_sem.at[slot],
            device_id={"ctx": target},
            device_id_type=pl.DeviceIdType.MESH,
        )

    def arrived(slot):
        pltpu.make_async_copy(o_ref.at[slot], o_ref.at[slot], recv_sem.at[slot]).wait()

    own = pltpu.make_async_copy(x_ref, o_ref.at[rank], own_sem)
    own.start()
    barrier = pltpu.get_barrier_semaphore()
    peers = [lax.rem(rank + 2 * j, ranks) for j in range(1, chips)]
    for target in peers + [other]:
        pl.semaphore_signal(
            barrier, inc=1, device_id={"ctx": target}, device_id_type=pl.DeviceIdType.MESH
        )
    pl.semaphore_wait(barrier, chips)
    sends = [send(x_ref, rank, send_sem.at[j], target) for j, target in enumerate(peers)]
    sends.append(send(x_ref, rank, send_sem.at[chips - 1], other))
    for copy in sends:
        copy.start()
    for j in range(1, chips):
        slot = lax.rem(rank + 2 * j, ranks)
        arrived(slot)
        copy = send(o_ref.at[slot], slot, pass_sem.at[j], other)
        copy.start()
        sends.append(copy)
    for j in range(chips):
        arrived(lax.rem(other + 2 * j, ranks))
    for copy in sends:
        copy.wait_send()
    own.wait()


def gather(packed):
    ranks = lax.axis_size("ctx")
    chips = ranks // 2
    out = pl.pallas_call(
        functools.partial(gather_kernel, ranks),
        out_shape=jax.ShapeDtypeStruct((ranks,) + packed.shape, packed.dtype),
        in_specs=[pl.BlockSpec(memory_space=pl.ANY)],
        out_specs=pl.BlockSpec(memory_space=pl.ANY),
        scratch_shapes=[
            pltpu.SemaphoreType.DMA,
            pltpu.SemaphoreType.DMA((chips,)),
            pltpu.SemaphoreType.DMA((chips,)),
            pltpu.SemaphoreType.DMA((ranks,)),
        ],
        compiler_params=pltpu.CompilerParams(collective_id=1, has_side_effects=True),
    )(packed)
    return out.reshape(ranks * packed.shape[0], packed.shape[1])


def project(first, queries, q_sc, packed, key_sc, mask_rows, out_weight, out_scale):
    n = lax.axis_size("head")
    ranks = lax.axis_size("ctx")
    rows, width = queries.shape
    chunks = rows // BLK
    features = out_weight.shape[1] // n
    vmem = pl.BlockSpec(memory_space=pltpu.VMEM)
    return pl.pallas_call(
        functools.partial(project_kernel, n, ranks),
        out_shape=jax.ShapeDtypeStruct((rows, features), jnp.bfloat16),
        in_specs=[vmem] * 6 + [pl.BlockSpec(memory_space=pl.ANY), vmem],
        out_specs=vmem,
        scratch_shapes=[
            pltpu.VMEM((n, width, features), jnp.bfloat16),
            pltpu.VMEM((chunks, BLK, width), jnp.bfloat16),
            pltpu.VMEM((chunks, n + 1, BLK, features), jnp.bfloat16),
            pltpu.VMEM((GROUP, BLK, HD), jnp.float32),
            pltpu.VMEM((GROUP, BLK, HD), jnp.float32),
            pltpu.VMEM((GROUP, BLK, 2 * HD), jnp.float32),
            pltpu.SemaphoreType.DMA((n,)),
            pltpu.SemaphoreType.DMA((chunks, n)),
            pltpu.SemaphoreType.DMA((chunks, n + 1)),
        ],
        compiler_params=pltpu.CompilerParams(
            collective_id=0, has_side_effects=True, vmem_limit_bytes=60 * 2**20
        ),
    )(first, queries, q_sc, packed, key_sc, mask_rows, out_weight, out_scale.reshape(1, -1))


def local(
    queries, query_scale, keys, key_scale, values, value_scale, block_mask, out_weight, out_scale
):
    rows = queries.shape[0]
    kv_local = keys.shape[1] // HD
    rank = lax.axis_index("ctx").astype(jnp.int32)
    scaled = (
        values.reshape(rows, kv_local, HD).astype(jnp.float32)
        * value_scale.astype(jnp.float32)[..., None]
    ).astype(jnp.bfloat16).reshape(rows, kv_local * HD)
    width = 2 * kv_local * HD
    slots = kv_local * (rows // BLK)
    tail = jnp.pad(key_scale.T.reshape(slots, BLK), ((0, PAD_ROWS - slots), (0, width - BLK)))
    packed = jnp.concatenate([jnp.concatenate([keys, scaled], axis=1), tail], axis=0)
    gathered = gather(packed)
    ranks = gathered.shape[0] // packed.shape[0]
    key_sc = gathered.reshape(ranks, rows + PAD_ROWS, width)[:, rows : rows + slots, :BLK]
    key_sc = jnp.transpose(key_sc.astype(jnp.float32).reshape(ranks, kv_local, rows), (1, 0, 2))
    key_sc = key_sc.reshape(kv_local, 1, ranks * rows)
    q_sc = jnp.transpose(query_scale.reshape(rows, kv_local, GROUP), (1, 0, 2))
    own = lax.dynamic_slice_in_dim(block_mask, rank * (rows // BLK), rows // BLK, 0)
    mask_rows = jnp.repeat(own, BLK, axis=1)[:, None, :]
    first = attend(queries, q_sc, gathered, key_sc, block_mask, rank, 1)
    return project(first, queries, q_sc, gathered, key_sc, mask_rows, out_weight, out_scale)


def solution(mesh):
    return jax.shard_map(
        local,
        mesh=mesh,
        in_specs=(
            P("ctx", "head"),
            P("ctx", "head"),
            P("ctx", "head"),
            P("ctx", "head"),
            P("ctx", "head"),
            P("ctx", "head"),
            P(),
            P("head", None),
            P("head"),
        ),
        out_specs=P("ctx", "head"),
        check_vma=False,
    )
```

```python
import functools
import math

import jax
import jax.numpy as jnp
from jax import lax
from jax.experimental import pallas as pl
from jax.experimental.pallas import tpu as pltpu
from jax.sharding import PartitionSpec as P

HD = 128
GROUP = 8
BLK = 128
PAD_ROWS = 16
NEG_FILL = -1e30


def attend_kernel(
    per_rank, mask_ref, rank_ref, q_ref, qs_ref, k_ref, v_ref, ks_ref, o_ref, order, factor, top, accum
):
    block = rank_ref[0] * per_rank + pl.program_id(1)
    stride = per_rank * BLK + PAD_ROWS

    def note(j, count):
        @pl.when(mask_ref[block, j] == 1)
        def _():
            order[count] = j

        return count + jnp.where(mask_ref[block, j] == 1, 1, 0)

    count = lax.fori_loop(0, block, note, jnp.int32(0))
    order[count] = block
    order[count + 1] = block
    padded = lax.rem(count, 2) == 0
    pairs = count // 2 + 1

    scale = math.log2(math.e) / math.sqrt(HD)
    for h in range(GROUP):
        column = qs_ref[0, :, h : h + 1].astype(jnp.float32) * scale
        factor[h] = jnp.broadcast_to(column, (BLK, HD))
    top[...] = jnp.full_like(top, NEG_FILL)
    accum[...] = jnp.zeros_like(accum)

    def rows_of(j):
        return pl.ds(pl.multiple_of((j // per_rank) * stride + lax.rem(j, per_rank) * BLK, PAD_ROWS), BLK)

    def step(pair, last):
        a, b = order[2 * pair], order[2 * pair + 1]
        keys = jnp.concatenate([k_ref[rows_of(a), :], k_ref[rows_of(b), :]], axis=0)
        vals = jnp.concatenate([v_ref[rows_of(a), :], v_ref[rows_of(b), :]], axis=0)
        vals = jnp.concatenate([vals, jnp.ones_like(vals)], axis=1)
        lanes = [pl.ds(pl.multiple_of(j * BLK, BLK), BLK) for j in (a, b)]
        key_sc = jnp.concatenate([ks_ref[0, :, lanes[0]], ks_ref[0, :, lanes[1]]], axis=1)
        if last:
            row = lax.broadcasted_iota(jnp.int32, (BLK, 2 * BLK), 0)
            col = lax.broadcasted_iota(jnp.int32, (BLK, 2 * BLK), 1)
            first_ok = jnp.where(padded, 0, BLK)
            allowed = (col < first_ok) | ((col >= BLK) & (col - BLK <= row))
        for h in range(GROUP):
            raw = lax.dot_general(
                q_ref[:, h * HD : (h + 1) * HD],
                keys,
                (((1,), (1,)), ((), ())),
                preferred_element_type=jnp.float32,
            )
            x = raw * key_sc
            if last:
                x = jnp.where(allowed, x, NEG_FILL)
            old = top[h]
            new = jnp.maximum(old, jnp.max(x, axis=1, keepdims=True))
            fac = factor[h]
            decay = jnp.exp2((old - new) * fac)
            expo = jnp.exp2(
                (x - jnp.concatenate([new, new], axis=1)) * jnp.concatenate([fac, fac], axis=1)
            )
            top[h] = new
            accum[h] = accum[h] * jnp.concatenate([decay, decay], axis=1) + jnp.dot(
                expo.astype(jnp.bfloat16), vals, preferred_element_type=jnp.float32
            )

    @pl.loop(0, pairs - 1)
    def _(pair):
        step(pair, False)

    step(pairs - 1, True)
    for h in range(GROUP):
        o_ref[:, h * HD : (h + 1) * HD] = (accum[h, :, :HD] / accum[h, :, HD:]).astype(jnp.bfloat16)


def attend(queries, q_sc, packed, key_sc, block_mask, rank, blocks):
    rows, width = queries.shape
    kv_local = width // (GROUP * HD)
    per_rank = rows // BLK
    count = block_mask.shape[0]
    return pl.pallas_call(
        functools.partial(attend_kernel, per_rank),
        out_shape=jax.ShapeDtypeStruct((blocks * BLK, width), jnp.bfloat16),
        grid_spec=pltpu.PrefetchScalarGridSpec(
            num_scalar_prefetch=2,
            grid=(kv_local, blocks),
            in_specs=[
                pl.BlockSpec((BLK, GROUP * HD), lambda g, i, *_: (i, g)),
                pl.BlockSpec((1, BLK, GROUP), lambda g, i, *_: (g, i, 0)),
                pl.BlockSpec((packed.shape[0], HD), lambda g, i, *_: (0, g)),
                pl.BlockSpec((packed.shape[0], HD), lambda g, i, *_: (0, kv_local + g)),
                pl.BlockSpec((1, 1, count * BLK), lambda g, i, *_: (g, 0, 0)),
            ],
            out_specs=pl.BlockSpec((BLK, GROUP * HD), lambda g, i, *_: (i, g)),
            scratch_shapes=[
                pltpu.SMEM((count + 2,), jnp.int32),
                pltpu.VMEM((GROUP, BLK, HD), jnp.float32),
                pltpu.VMEM((GROUP, BLK, HD), jnp.float32),
                pltpu.VMEM((GROUP, BLK, 2 * HD), jnp.float32),
            ],
        ),
        compiler_params=pltpu.CompilerParams(vmem_limit_bytes=24 * 2**20),
    )(block_mask, rank.reshape(1), queries, q_sc, packed, packed, key_sc)


def project_kernel(
    n,
    ranks,
    first_ref,
    q_ref,
    qs_ref,
    kv_ref,
    ks_ref,
    mask_ref,
    w_hbm,
    scale_ref,
    o_ref,
    weight,
    attended,
    parts,
    factor,
    top,
    accum,
    w_sem,
    send_sem,
    recv_sem,
):
    me = lax.axis_index("head")
    rank = lax.axis_index("ctx")
    chunks = attended.shape[0]
    done = first_ref.shape[0] // BLK
    kv_local = qs_ref.shape[0]
    stride = chunks * BLK + PAD_ROWS
    features = weight.shape[2]
    tile = math.gcd(features, 512)
    is_end = (me == 0) | (me == n - 1)

    def load_weight(d):
        return pltpu.make_async_copy(
            w_hbm.at[:, pl.ds(pl.multiple_of(d * features, features), features)],
            weight.at[d],
            w_sem.at[d],
        )

    load_weight(jnp.where(me < (n + 1) // 2, n - 1, 0)).start()

    @pl.when(jnp.logical_not(is_end))
    def _():
        for s in range(1, n):
            load_weight(jnp.where(me < (n + 1) // 2, n - 1 - s, s)).start()

    barrier = pltpu.get_barrier_semaphore()

    @pl.when(me > 0)
    def _():
        pl.semaphore_signal(
            barrier, inc=1, device_id={"head": me - 1}, device_id_type=pl.DeviceIdType.MESH
        )

    @pl.when(me < n - 1)
    def _():
        pl.semaphore_signal(
            barrier, inc=1, device_id={"head": me + 1}, device_id_type=pl.DeviceIdType.MESH
        )

    @pl.when(is_end)
    def _():
        pl.semaphore_wait(barrier, 1)

    @pl.when(jnp.logical_not(is_end))
    def _():
        pl.semaphore_wait(barrier, 2)

    for c in range(done):
        attended[c] = first_ref[c * BLK : (c + 1) * BLK, :]

    def attend_chunk(t):
        block = rank * chunks + t
        q_rows = pl.ds(pl.multiple_of(t * BLK, BLK), BLK)
        scale = math.log2(math.e) / math.sqrt(HD)

        @pl.loop(0, kv_local)
        def _(g):
            for h in range(GROUP):
                column = qs_ref[g, q_rows, h : h + 1].astype(jnp.float32) * scale
                factor[h] = jnp.broadcast_to(column, (BLK, HD))
            top[...] = jnp.full_like(top, NEG_FILL)
            accum[...] = jnp.zeros_like(accum)

            @pl.loop(0, block // 2 + 1)
            def _(pair):
                a = 2 * pair
                b = jnp.minimum(a + 1, ranks * chunks - 1)

                def piece(j, column):
                    begin = (j // chunks) * stride + lax.rem(j, chunks) * BLK
                    return kv_ref[
                        pl.ds(pl.multiple_of(begin, PAD_ROWS), BLK),
                        pl.ds(pl.multiple_of(column * HD, HD), HD),
                    ]

                def lanes(j):
                    return pl.ds(pl.multiple_of(j * BLK, BLK), BLK)

                keys = jnp.concatenate([piece(a, g), piece(b, g)], axis=0)
                vals = jnp.concatenate([piece(a, kv_local + g), piece(b, kv_local + g)], axis=0)
                vals = jnp.concatenate([vals, jnp.ones_like(vals)], axis=1)
                key_sc = jnp.concatenate([ks_ref[g, :, lanes(a)], ks_ref[g, :, lanes(b)]], axis=1)
                read = jnp.concatenate([mask_ref[t, :, lanes(a)], mask_ref[t, :, lanes(b)]], axis=1)
                row = lax.broadcasted_iota(jnp.int32, (BLK, 2 * BLK), 0) + block * BLK
                col = lax.broadcasted_iota(jnp.int32, (BLK, 2 * BLK), 1) + a * BLK
                allowed = (jnp.broadcast_to(read, (BLK, 2 * BLK)) == 1) & (col <= row)
                for h in range(GROUP):
                    column = pl.multiple_of((g * GROUP + h) * HD, HD)
                    raw = lax.dot_general(
                        q_ref[q_rows, pl.ds(column, HD)],
                        keys,
                        (((1,), (1,)), ((), ())),
                        preferred_element_type=jnp.float32,
                    )
                    x = jnp.where(allowed, raw * key_sc, NEG_FILL)
                    old = top[h]
                    new = jnp.maximum(old, jnp.max(x, axis=1, keepdims=True))
                    fac = factor[h]
                    decay = jnp.exp2((old - new) * fac)
                    expo = jnp.exp2(
                        (x - jnp.concatenate([new, new], axis=1))
                        * jnp.concatenate([fac, fac], axis=1)
                    )
                    top[h] = new
                    accum[h] = accum[h] * jnp.concatenate([decay, decay], axis=1) + jnp.dot(
                        expo.astype(jnp.bfloat16), vals, preferred_element_type=jnp.float32
                    )

            for h in range(GROUP):
                column = pl.multiple_of((g * GROUP + h) * HD, HD)
                attended[t, :, pl.ds(column, HD)] = (
                    accum[h, :, :HD] / accum[h, :, HD:]
                ).astype(jnp.bfloat16)

    def products(c, d, use):
        @pl.loop(0, features // tile)
        def _(i):
            cols = pl.ds(pl.multiple_of(i * tile, tile), tile)
            use(
                cols,
                jnp.dot(attended[c], weight[d, :, cols], preferred_element_type=jnp.float32),
            )

    def hop(c, d, up):
        slot = d if up else jnp.where(d == me - 1, n, d)
        return pltpu.make_async_remote_copy(
            src_ref=parts.at[c, d],
            dst_ref=parts.at[c, slot],
            send_sem=send_sem.at[c, d],
            recv_sem=recv_sem.at[c, slot],
            device_id={"head": me + 1 if up else me - 1},
            device_id_type=pl.DeviceIdType.MESH,
        )

    def arrived(c, slot):
        pltpu.make_async_copy(parts.at[c, slot], parts.at[c, slot], recv_sem.at[c, slot]).wait()

    def count_of(up):
        return n - 1 - me if up else me

    def nth(q, up):
        per = jnp.maximum(count_of(up), 1)
        k = lax.rem(q, per)
        return hop(lax.div(q, per), n - 1 - k if up else k, up)

    def relay(c, k, up):
        d = n - 1 - k if up else k
        source = me > 0 if up else me < n - 1

        @pl.when(c == 0)
        def _():
            load_weight(d).wait()

            @pl.when(is_end)
            def _():
                load_weight(d - 1 if up else d + 1).start()

        @pl.when(source)
        def _():
            arrived(c, d)

            def use(cols, product):
                parts[c, d, :, cols] = (parts[c, d, :, cols].astype(jnp.float32) + product).astype(
                    jnp.bfloat16
                )

            products(c, d, use)

        @pl.when(jnp.logical_not(source))
        def _():
            def use(cols, product):
                parts[c, d, :, cols] = product.astype(jnp.bfloat16)

            products(c, d, use)

        q = c * count_of(up) + k

        final = c == chunks - 1

        @pl.when((q >= 2) & (jnp.logical_not(final) | (k == 0)))
        def _():
            nth(q - 2, up).wait_send()

        @pl.when((q >= 1) & final)
        def _():
            nth(q - 1, up).wait_send()

        nth(q, up).start()

    def forward(c):
        def ups():
            @pl.loop(0, n - 1 - me)
            def _(k):
                relay(c, k, True)

        def downs():
            @pl.loop(0, me)
            def _(k):
                relay(c, k, False)

        @pl.when(me < n // 2)
        def _():
            ups()
            downs()

        @pl.when(me >= n // 2)
        def _():
            downs()
            ups()

    @pl.loop(0, chunks)
    def _(t):
        @pl.when(t >= done)
        def _():
            attend_chunk(t)

        @pl.when(is_end)
        def _():
            forward(t)

        @pl.when(jnp.logical_not(is_end) & (t > 0))
        def _():
            forward(t - 1)

    @pl.when(jnp.logical_not(is_end))
    def _():
        forward(chunks - 1)

    load_weight(me).wait()

    @pl.loop(0, chunks)
    def _(c):
        rows = pl.ds(pl.multiple_of(c * BLK, BLK), BLK)

        def finish(below, above):
            if below:
                arrived(c, me)
            if above:
                arrived(c, n)

            def use(cols, product):
                if below:
                    product = product + parts[c, me, :, cols].astype(jnp.float32)
                if above:
                    product = product + parts[c, n, :, cols].astype(jnp.float32)
                o_ref[rows, cols] = (product * scale_ref[:, cols]).astype(jnp.bfloat16)

            products(c, me, use)

        @pl.when(me == 0)
        def _():
            finish(False, True)

        @pl.when(me == n - 1)
        def _():
            finish(True, False)

        @pl.when(jnp.logical_not(is_end))
        def _():
            finish(True, True)

    for up in (True, False):
        total = chunks * count_of(up)

        @pl.when(total > 0)
        def _():
            nth(total - 1, up).wait_send()


def gather_kernel(ranks, x_ref, o_ref, own_sem, send_sem, pass_sem, recv_sem):
    rank = lax.axis_index("ctx")
    chips = ranks // 2
    other = rank + 1 - 2 * lax.rem(rank, 2)

    def send(src, slot, sem, target):
        return pltpu.make_async_remote_copy(
            src_ref=src,
            dst_ref=o_ref.at[slot],
            send_sem=sem,
            recv_sem=recv_sem.at[slot],
            device_id={"ctx": target},
            device_id_type=pl.DeviceIdType.MESH,
        )

    def arrived(slot):
        pltpu.make_async_copy(o_ref.at[slot], o_ref.at[slot], recv_sem.at[slot]).wait()

    own = pltpu.make_async_copy(x_ref, o_ref.at[rank], own_sem)
    own.start()
    barrier = pltpu.get_barrier_semaphore()
    peers = [lax.rem(rank + 2 * j, ranks) for j in range(1, chips)]
    for target in peers + [other]:
        pl.semaphore_signal(
            barrier, inc=1, device_id={"ctx": target}, device_id_type=pl.DeviceIdType.MESH
        )
    pl.semaphore_wait(barrier, chips)
    sends = [send(x_ref, rank, send_sem.at[j], target) for j, target in enumerate(peers)]
    sends.append(send(x_ref, rank, send_sem.at[chips - 1], other))
    for copy in sends:
        copy.start()
    for j in range(1, chips):
        slot = lax.rem(rank + 2 * j, ranks)
        arrived(slot)
        copy = send(o_ref.at[slot], slot, pass_sem.at[j], other)
        copy.start()
        sends.append(copy)
    for j in range(chips):
        arrived(lax.rem(other + 2 * j, ranks))
    for copy in sends:
        copy.wait_send()
    own.wait()


def gather(packed):
    ranks = lax.axis_size("ctx")
    chips = ranks // 2
    out = pl.pallas_call(
        functools.partial(gather_kernel, ranks),
        out_shape=jax.ShapeDtypeStruct((ranks,) + packed.shape, packed.dtype),
        in_specs=[pl.BlockSpec(memory_space=pl.ANY)],
        out_specs=pl.BlockSpec(memory_space=pl.ANY),
        scratch_shapes=[
            pltpu.SemaphoreType.DMA,
            pltpu.SemaphoreType.DMA((chips,)),
            pltpu.SemaphoreType.DMA((chips,)),
            pltpu.SemaphoreType.DMA((ranks,)),
        ],
        compiler_params=pltpu.CompilerParams(collective_id=1, has_side_effects=True),
    )(packed)
    return out.reshape(ranks * packed.shape[0], packed.shape[1])


def project(first, queries, q_sc, packed, key_sc, mask_rows, out_weight, out_scale):
    n = lax.axis_size("head")
    ranks = lax.axis_size("ctx")
    rows, width = queries.shape
    chunks = rows // BLK
    features = out_weight.shape[1] // n
    vmem = pl.BlockSpec(memory_space=pltpu.VMEM)
    return pl.pallas_call(
        functools.partial(project_kernel, n, ranks),
        out_shape=jax.ShapeDtypeStruct((rows, features), jnp.bfloat16),
        in_specs=[vmem] * 6 + [pl.BlockSpec(memory_space=pl.ANY), vmem],
        out_specs=vmem,
        scratch_shapes=[
            pltpu.VMEM((n, width, features), jnp.bfloat16),
            pltpu.VMEM((chunks, BLK, width), jnp.bfloat16),
            pltpu.VMEM((chunks, n + 1, BLK, features), jnp.bfloat16),
            pltpu.VMEM((GROUP, BLK, HD), jnp.float32),
            pltpu.VMEM((GROUP, BLK, HD), jnp.float32),
            pltpu.VMEM((GROUP, BLK, 2 * HD), jnp.float32),
            pltpu.SemaphoreType.DMA((n,)),
            pltpu.SemaphoreType.DMA((chunks, n)),
            pltpu.SemaphoreType.DMA((chunks, n + 1)),
        ],
        compiler_params=pltpu.CompilerParams(
            collective_id=0, has_side_effects=True, vmem_limit_bytes=60 * 2**20
        ),
    )(first, queries, q_sc, packed, key_sc, mask_rows, out_weight, out_scale.reshape(1, -1))


def local(
    queries, query_scale, keys, key_scale, values, value_scale, block_mask, out_weight, out_scale
):
    rows = queries.shape[0]
    kv_local = keys.shape[1] // HD
    rank = lax.axis_index("ctx").astype(jnp.int32)
    scaled = (
        values.reshape(rows, kv_local, HD).astype(jnp.float32)
        * value_scale.astype(jnp.float32)[..., None]
    ).astype(jnp.bfloat16).reshape(rows, kv_local * HD)
    width = 2 * kv_local * HD
    slots = kv_local * (rows // BLK)
    tail = jnp.pad(key_scale.T.reshape(slots, BLK), ((0, PAD_ROWS - slots), (0, width - BLK)))
    packed = jnp.concatenate([jnp.concatenate([keys, scaled], axis=1), tail], axis=0)
    gathered = gather(packed)
    ranks = gathered.shape[0] // packed.shape[0]
    key_sc = gathered.reshape(ranks, rows + PAD_ROWS, width)[:, rows : rows + slots, :BLK]
    key_sc = jnp.transpose(key_sc.astype(jnp.float32).reshape(ranks, kv_local, rows), (1, 0, 2))
    key_sc = key_sc.reshape(kv_local, 1, ranks * rows)
    q_sc = jnp.transpose(query_scale.reshape(rows, kv_local, GROUP), (1, 0, 2))
    own = lax.dynamic_slice_in_dim(block_mask, rank * (rows // BLK), rows // BLK, 0)
    mask_rows = jnp.repeat(own, BLK, axis=1)[:, None, :]
    first = attend(queries, q_sc, gathered, key_sc, block_mask, rank, 1)
    return project(first, queries, q_sc, gathered, key_sc, mask_rows, out_weight, out_scale)


def solution(mesh):
    return jax.shard_map(
        local,
        mesh=mesh,
        in_specs=(
            P("ctx", "head"),
            P("ctx", "head"),
            P("ctx", "head"),
            P("ctx", "head"),
            P("ctx", "head"),
            P("ctx", "head"),
            P(),
            P("head", None),
            P("head"),
        ),
        out_specs=P("ctx", "head"),
        check_vma=False,
    )
```

```python
import functools
import math

import jax
import jax.numpy as jnp
from jax import lax
from jax.experimental import pallas as pl
from jax.experimental.pallas import tpu as pltpu
from jax.sharding import PartitionSpec as P

HD = 128
GROUP = 8
BLK = 128
PAD_ROWS = 16
HALVES = 2
DEPTH = 4
LAST = 2
NEG_FILL = -1e30


def attend_kernel(
    per_rank, mask_ref, rank_ref, q_ref, qs_ref, k_ref, v_ref, ks_ref, o_ref, order, factor, top, accum
):
    block = rank_ref[0] * per_rank + pl.program_id(1)
    stride = per_rank * BLK + PAD_ROWS

    def note(j, count):
        @pl.when(mask_ref[block, j] == 1)
        def _():
            order[count] = j

        return count + jnp.where(mask_ref[block, j] == 1, 1, 0)

    count = lax.fori_loop(0, block, note, jnp.int32(0))
    order[count] = block
    order[count + 1] = block
    padded = lax.rem(count, 2) == 0
    pairs = count // 2 + 1

    scale = math.log2(math.e) / math.sqrt(HD)
    for h in range(GROUP):
        column = qs_ref[0, :, h : h + 1].astype(jnp.float32) * scale
        factor[h] = jnp.broadcast_to(column, (BLK, HD))
    top[...] = jnp.full_like(top, NEG_FILL)
    accum[...] = jnp.zeros_like(accum)

    def rows_of(j):
        return pl.ds(pl.multiple_of((j // per_rank) * stride + lax.rem(j, per_rank) * BLK, PAD_ROWS), BLK)

    def step(pair, last):
        a, b = order[2 * pair], order[2 * pair + 1]
        keys = jnp.concatenate([k_ref[rows_of(a), :], k_ref[rows_of(b), :]], axis=0)
        vals = jnp.concatenate([v_ref[rows_of(a), :], v_ref[rows_of(b), :]], axis=0)
        vals = jnp.concatenate([vals, jnp.ones_like(vals)], axis=1)
        lanes = [pl.ds(pl.multiple_of(j * BLK, BLK), BLK) for j in (a, b)]
        key_sc = jnp.concatenate([ks_ref[0, :, lanes[0]], ks_ref[0, :, lanes[1]]], axis=1)
        if last:
            row = lax.broadcasted_iota(jnp.int32, (BLK, 2 * BLK), 0)
            col = lax.broadcasted_iota(jnp.int32, (BLK, 2 * BLK), 1)
            first_ok = jnp.where(padded, 0, BLK)
            allowed = (col < first_ok) | ((col >= BLK) & (col - BLK <= row))
        for h in range(GROUP):
            raw = lax.dot_general(
                q_ref[:, h * HD : (h + 1) * HD],
                keys,
                (((1,), (1,)), ((), ())),
                preferred_element_type=jnp.float32,
            )
            x = raw * key_sc
            if last:
                x = jnp.where(allowed, x, NEG_FILL)
            old = top[h]
            new = jnp.maximum(old, jnp.max(x, axis=1, keepdims=True))
            fac = factor[h]
            decay = jnp.exp2((old - new) * fac)
            expo = jnp.exp2(
                (x - jnp.concatenate([new, new], axis=1)) * jnp.concatenate([fac, fac], axis=1)
            )
            top[h] = new
            accum[h] = accum[h] * jnp.concatenate([decay, decay], axis=1) + jnp.dot(
                expo.astype(jnp.bfloat16), vals, preferred_element_type=jnp.float32
            )

    @pl.loop(0, pairs - 1)
    def _(pair):
        step(pair, False)

    step(pairs - 1, True)
    for h in range(GROUP):
        o_ref[:, h * HD : (h + 1) * HD] = (accum[h, :, :HD] / accum[h, :, HD:]).astype(jnp.bfloat16)


def attend(queries, q_sc, packed, key_sc, block_mask, rank, blocks):
    rows, width = queries.shape
    kv_local = width // (GROUP * HD)
    per_rank = rows // BLK
    count = block_mask.shape[0]
    return pl.pallas_call(
        functools.partial(attend_kernel, per_rank),
        out_shape=jax.ShapeDtypeStruct((blocks * BLK, width), jnp.bfloat16),
        grid_spec=pltpu.PrefetchScalarGridSpec(
            num_scalar_prefetch=2,
            grid=(kv_local, blocks),
            in_specs=[
                pl.BlockSpec((BLK, GROUP * HD), lambda g, i, *_: (i, g)),
                pl.BlockSpec((1, BLK, GROUP), lambda g, i, *_: (g, i, 0)),
                pl.BlockSpec((packed.shape[0], HD), lambda g, i, *_: (0, g)),
                pl.BlockSpec((packed.shape[0], HD), lambda g, i, *_: (0, kv_local + g)),
                pl.BlockSpec((1, 1, count * BLK), lambda g, i, *_: (g, 0, 0)),
            ],
            out_specs=pl.BlockSpec((BLK, GROUP * HD), lambda g, i, *_: (i, g)),
            scratch_shapes=[
                pltpu.SMEM((count + 2,), jnp.int32),
                pltpu.VMEM((GROUP, BLK, HD), jnp.float32),
                pltpu.VMEM((GROUP, BLK, HD), jnp.float32),
                pltpu.VMEM((GROUP, BLK, 2 * HD), jnp.float32),
            ],
        ),
        compiler_params=pltpu.CompilerParams(vmem_limit_bytes=24 * 2**20),
    )(block_mask, rank.reshape(1), queries, q_sc, packed, packed, key_sc)


def project_kernel(
    n,
    ranks,
    first_ref,
    q_ref,
    qs_ref,
    kv_ref,
    ks_ref,
    mask_ref,
    w_hbm,
    scale_ref,
    o_ref,
    weight,
    attended,
    parts,
    factor,
    top,
    accum,
    w_sem,
    send_sem,
    recv_sem,
):
    me = lax.axis_index("head")
    rank = lax.axis_index("ctx")
    chunks = attended.shape[0]
    done = first_ref.shape[0] // BLK
    kv_local = qs_ref.shape[0]
    stride = chunks * BLK + PAD_ROWS
    features = weight.shape[2]
    span = features // HALVES
    tile = math.gcd(span, 512)
    is_end = (me == 0) | (me == n - 1)

    def load_weight(d):
        return pltpu.make_async_copy(
            w_hbm.at[:, pl.ds(pl.multiple_of(d * features, features), features)],
            weight.at[d],
            w_sem.at[d],
        )

    load_weight(jnp.where(me < (n + 1) // 2, n - 1, 0)).start()

    @pl.when(jnp.logical_not(is_end))
    def _():
        for s in range(1, n):
            load_weight(jnp.where(me < (n + 1) // 2, n - 1 - s, s)).start()

    barrier = pltpu.get_barrier_semaphore()

    @pl.when(me > 0)
    def _():
        pl.semaphore_signal(
            barrier, inc=1, device_id={"head": me - 1}, device_id_type=pl.DeviceIdType.MESH
        )

    @pl.when(me < n - 1)
    def _():
        pl.semaphore_signal(
            barrier, inc=1, device_id={"head": me + 1}, device_id_type=pl.DeviceIdType.MESH
        )

    @pl.when(is_end)
    def _():
        pl.semaphore_wait(barrier, 1)

    @pl.when(jnp.logical_not(is_end))
    def _():
        pl.semaphore_wait(barrier, 2)

    for c in range(done):
        attended[c] = first_ref[c * BLK : (c + 1) * BLK, :]

    def attend_chunk(t):
        block = rank * chunks + t
        q_rows = pl.ds(pl.multiple_of(t * BLK, BLK), BLK)
        scale = math.log2(math.e) / math.sqrt(HD)

        @pl.loop(0, kv_local)
        def _(g):
            for h in range(GROUP):
                column = qs_ref[g, q_rows, h : h + 1].astype(jnp.float32) * scale
                factor[h] = jnp.broadcast_to(column, (BLK, HD))
            top[...] = jnp.full_like(top, NEG_FILL)
            accum[...] = jnp.zeros_like(accum)

            @pl.loop(0, block // 2 + 1)
            def _(pair):
                a = 2 * pair
                b = jnp.minimum(a + 1, ranks * chunks - 1)

                def piece(j, column):
                    begin = (j // chunks) * stride + lax.rem(j, chunks) * BLK
                    return kv_ref[
                        pl.ds(pl.multiple_of(begin, PAD_ROWS), BLK),
                        pl.ds(pl.multiple_of(column * HD, HD), HD),
                    ]

                def lanes(j):
                    return pl.ds(pl.multiple_of(j * BLK, BLK), BLK)

                keys = jnp.concatenate([piece(a, g), piece(b, g)], axis=0)
                vals = jnp.concatenate([piece(a, kv_local + g), piece(b, kv_local + g)], axis=0)
                vals = jnp.concatenate([vals, jnp.ones_like(vals)], axis=1)
                key_sc = jnp.concatenate([ks_ref[g, :, lanes(a)], ks_ref[g, :, lanes(b)]], axis=1)
                read = jnp.concatenate([mask_ref[t, :, lanes(a)], mask_ref[t, :, lanes(b)]], axis=1)
                row = lax.broadcasted_iota(jnp.int32, (BLK, 2 * BLK), 0) + block * BLK
                col = lax.broadcasted_iota(jnp.int32, (BLK, 2 * BLK), 1) + a * BLK
                allowed = (jnp.broadcast_to(read, (BLK, 2 * BLK)) == 1) & (col <= row)
                for h in range(GROUP):
                    column = pl.multiple_of((g * GROUP + h) * HD, HD)
                    raw = lax.dot_general(
                        q_ref[q_rows, pl.ds(column, HD)],
                        keys,
                        (((1,), (1,)), ((), ())),
                        preferred_element_type=jnp.float32,
                    )
                    x = jnp.where(allowed, raw * key_sc, NEG_FILL)
                    old = top[h]
                    new = jnp.maximum(old, jnp.max(x, axis=1, keepdims=True))
                    fac = factor[h]
                    decay = jnp.exp2((old - new) * fac)
                    expo = jnp.exp2(
                        (x - jnp.concatenate([new, new], axis=1))
                        * jnp.concatenate([fac, fac], axis=1)
                    )
                    top[h] = new
                    accum[h] = accum[h] * jnp.concatenate([decay, decay], axis=1) + jnp.dot(
                        expo.astype(jnp.bfloat16), vals, preferred_element_type=jnp.float32
                    )

            for h in range(GROUP):
                column = pl.multiple_of((g * GROUP + h) * HD, HD)
                attended[t, :, pl.ds(column, HD)] = (
                    accum[h, :, :HD] / accum[h, :, HD:]
                ).astype(jnp.bfloat16)

    def products(c, d, half, use):
        @pl.loop(0, span // tile)
        def _(i):
            cols = pl.ds(pl.multiple_of(i * tile, tile), tile)
            whole = pl.ds(pl.multiple_of(half * span + i * tile, tile), tile)
            use(
                cols,
                whole,
                jnp.dot(attended[c], weight[d, :, whole], preferred_element_type=jnp.float32),
            )

    def hop(c, d, half, up):
        slot = d if up else jnp.where(d == me - 1, n, d)
        return pltpu.make_async_remote_copy(
            src_ref=parts.at[c, d, half],
            dst_ref=parts.at[c, slot, half],
            send_sem=send_sem.at[c, d, half],
            recv_sem=recv_sem.at[c, slot, half],
            device_id={"head": me + 1 if up else me - 1},
            device_id_type=pl.DeviceIdType.MESH,
        )

    def arrived(c, slot, half):
        piece = parts.at[c, slot, half]
        pltpu.make_async_copy(piece, piece, recv_sem.at[c, slot, half]).wait()

    def count_of(up):
        return HALVES * (n - 1 - me if up else me)

    def nth(q, up):
        per = jnp.maximum(count_of(up), 1)
        k = lax.rem(q, per)
        j = lax.div(k, HALVES)
        return hop(lax.div(q, per), n - 1 - j if up else j, lax.rem(k, HALVES), up)

    def relay(c, k, up):
        j = lax.div(k, HALVES)
        half = lax.rem(k, HALVES)
        d = n - 1 - j if up else j
        source = me > 0 if up else me < n - 1

        @pl.when((c == 0) & (half == 0))
        def _():
            load_weight(d).wait()

            @pl.when(is_end)
            def _():
                load_weight(d - 1 if up else d + 1).start()

        @pl.when(source)
        def _():
            arrived(c, d, half)

            def use(cols, whole, product):
                parts[c, d, half, :, cols] = (
                    parts[c, d, half, :, cols].astype(jnp.float32) + product
                ).astype(jnp.bfloat16)

            products(c, d, half, use)

        @pl.when(jnp.logical_not(source))
        def _():
            def use(cols, whole, product):
                parts[c, d, half, :, cols] = product.astype(jnp.bfloat16)

            products(c, d, half, use)

        q = c * count_of(up) + k
        final = c == chunks - 1

        @pl.when((q >= DEPTH) & (jnp.logical_not(final) | (k < LAST)))
        def _():
            nth(q - DEPTH, up).wait_send()

        @pl.when((q >= LAST) & final)
        def _():
            nth(q - LAST, up).wait_send()

        nth(q, up).start()

    def forward(c):
        def ups():
            @pl.loop(0, count_of(True))
            def _(k):
                relay(c, k, True)

        def downs():
            @pl.loop(0, count_of(False))
            def _(k):
                relay(c, k, False)

        @pl.when(me < n // 2)
        def _():
            ups()
            downs()

        @pl.when(me >= n // 2)
        def _():
            downs()
            ups()

    @pl.loop(0, chunks)
    def _(t):
        @pl.when(t >= done)
        def _():
            attend_chunk(t)

        @pl.when(is_end)
        def _():
            forward(t)

        @pl.when(jnp.logical_not(is_end) & (t > 0))
        def _():
            forward(t - 1)

    @pl.when(jnp.logical_not(is_end))
    def _():
        forward(chunks - 1)

    load_weight(me).wait()

    @pl.loop(0, chunks)
    def _(c):
        rows = pl.ds(pl.multiple_of(c * BLK, BLK), BLK)

        def finish(below, above):
            @pl.loop(0, HALVES)
            def _(half):
                if below:
                    arrived(c, me, half)
                if above:
                    arrived(c, n, half)

                def use(cols, whole, product):
                    if below:
                        product = product + parts[c, me, half, :, cols].astype(jnp.float32)
                    if above:
                        product = product + parts[c, n, half, :, cols].astype(jnp.float32)
                    o_ref[rows, whole] = (product * scale_ref[:, whole]).astype(jnp.bfloat16)

                products(c, me, half, use)

        @pl.when(me == 0)
        def _():
            finish(False, True)

        @pl.when(me == n - 1)
        def _():
            finish(True, False)

        @pl.when(jnp.logical_not(is_end))
        def _():
            finish(True, True)

    for up in (True, False):
        total = chunks * count_of(up)

        @pl.loop(jnp.maximum(total - LAST, 0), total)
        def _(q):
            nth(q, up).wait_send()


def gather_kernel(ranks, x_ref, o_ref, own_sem, send_sem, pass_sem, recv_sem):
    rank = lax.axis_index("ctx")
    chips = ranks // 2
    other = rank + 1 - 2 * lax.rem(rank, 2)

    def send(src, slot, sem, target):
        return pltpu.make_async_remote_copy(
            src_ref=src,
            dst_ref=o_ref.at[slot],
            send_sem=sem,
            recv_sem=recv_sem.at[slot],
            device_id={"ctx": target},
            device_id_type=pl.DeviceIdType.MESH,
        )

    def arrived(slot):
        pltpu.make_async_copy(o_ref.at[slot], o_ref.at[slot], recv_sem.at[slot]).wait()

    own = pltpu.make_async_copy(x_ref, o_ref.at[rank], own_sem)
    own.start()
    barrier = pltpu.get_barrier_semaphore()
    peers = [lax.rem(rank + 2 * j, ranks) for j in range(1, chips)]
    for target in peers + [other]:
        pl.semaphore_signal(
            barrier, inc=1, device_id={"ctx": target}, device_id_type=pl.DeviceIdType.MESH
        )
    pl.semaphore_wait(barrier, chips)
    sends = [send(x_ref, rank, send_sem.at[j], target) for j, target in enumerate(peers)]
    sends.append(send(x_ref, rank, send_sem.at[chips - 1], other))
    for copy in sends:
        copy.start()
    for j in range(1, chips):
        slot = lax.rem(rank + 2 * j, ranks)
        arrived(slot)
        copy = send(o_ref.at[slot], slot, pass_sem.at[j], other)
        copy.start()
        sends.append(copy)
    for j in range(chips):
        arrived(lax.rem(other + 2 * j, ranks))
    for copy in sends:
        copy.wait_send()
    own.wait()


def gather(packed):
    ranks = lax.axis_size("ctx")
    chips = ranks // 2
    out = pl.pallas_call(
        functools.partial(gather_kernel, ranks),
        out_shape=jax.ShapeDtypeStruct((ranks,) + packed.shape, packed.dtype),
        in_specs=[pl.BlockSpec(memory_space=pl.ANY)],
        out_specs=pl.BlockSpec(memory_space=pl.ANY),
        scratch_shapes=[
            pltpu.SemaphoreType.DMA,
            pltpu.SemaphoreType.DMA((chips,)),
            pltpu.SemaphoreType.DMA((chips,)),
            pltpu.SemaphoreType.DMA((ranks,)),
        ],
        compiler_params=pltpu.CompilerParams(collective_id=1, has_side_effects=True),
    )(packed)
    return out.reshape(ranks * packed.shape[0], packed.shape[1])


def project(first, queries, q_sc, packed, key_sc, mask_rows, out_weight, out_scale):
    n = lax.axis_size("head")
    ranks = lax.axis_size("ctx")
    rows, width = queries.shape
    chunks = rows // BLK
    features = out_weight.shape[1] // n
    vmem = pl.BlockSpec(memory_space=pltpu.VMEM)
    return pl.pallas_call(
        functools.partial(project_kernel, n, ranks),
        out_shape=jax.ShapeDtypeStruct((rows, features), jnp.bfloat16),
        in_specs=[vmem] * 6 + [pl.BlockSpec(memory_space=pl.ANY), vmem],
        out_specs=vmem,
        scratch_shapes=[
            pltpu.VMEM((n, width, features), jnp.bfloat16),
            pltpu.VMEM((chunks, BLK, width), jnp.bfloat16),
            pltpu.VMEM((chunks, n + 1, HALVES, BLK, features // HALVES), jnp.bfloat16),
            pltpu.VMEM((GROUP, BLK, HD), jnp.float32),
            pltpu.VMEM((GROUP, BLK, HD), jnp.float32),
            pltpu.VMEM((GROUP, BLK, 2 * HD), jnp.float32),
            pltpu.SemaphoreType.DMA((n,)),
            pltpu.SemaphoreType.DMA((chunks, n, HALVES)),
            pltpu.SemaphoreType.DMA((chunks, n + 1, HALVES)),
        ],
        compiler_params=pltpu.CompilerParams(
            collective_id=0, has_side_effects=True, vmem_limit_bytes=60 * 2**20
        ),
    )(first, queries, q_sc, packed, key_sc, mask_rows, out_weight, out_scale.reshape(1, -1))


def local(
    queries, query_scale, keys, key_scale, values, value_scale, block_mask, out_weight, out_scale
):
    rows = queries.shape[0]
    kv_local = keys.shape[1] // HD
    rank = lax.axis_index("ctx").astype(jnp.int32)
    scaled = (
        values.reshape(rows, kv_local, HD).astype(jnp.float32)
        * value_scale.astype(jnp.float32)[..., None]
    ).astype(jnp.bfloat16).reshape(rows, kv_local * HD)
    width = 2 * kv_local * HD
    slots = kv_local * (rows // BLK)
    tail = jnp.pad(key_scale.T.reshape(slots, BLK), ((0, PAD_ROWS - slots), (0, width - BLK)))
    packed = jnp.concatenate([jnp.concatenate([keys, scaled], axis=1), tail], axis=0)
    gathered = gather(packed)
    ranks = gathered.shape[0] // packed.shape[0]
    key_sc = gathered.reshape(ranks, rows + PAD_ROWS, width)[:, rows : rows + slots, :BLK]
    key_sc = jnp.transpose(key_sc.astype(jnp.float32).reshape(ranks, kv_local, rows), (1, 0, 2))
    key_sc = key_sc.reshape(kv_local, 1, ranks * rows)
    q_sc = jnp.transpose(query_scale.reshape(rows, kv_local, GROUP), (1, 0, 2))
    own = lax.dynamic_slice_in_dim(block_mask, rank * (rows // BLK), rows // BLK, 0)
    mask_rows = jnp.repeat(own, BLK, axis=1)[:, None, :]
    first = attend(queries, q_sc, gathered, key_sc, block_mask, rank, 1)
    return project(first, queries, q_sc, gathered, key_sc, mask_rows, out_weight, out_scale)


def solution(mesh):
    return jax.shard_map(
        local,
        mesh=mesh,
        in_specs=(
            P("ctx", "head"),
            P("ctx", "head"),
            P("ctx", "head"),
            P("ctx", "head"),
            P("ctx", "head"),
            P("ctx", "head"),
            P(),
            P("head", None),
            P("head"),
        ),
        out_specs=P("ctx", "head"),
        check_vma=False,
    )
```
